32 devices in a mesh: row: 4 (over y, x), col: 8 (over z, core).
Axes of the slice: x: 2, y: 2, z: 4, core: 2. Of those that a mesh axis runs over, the one named last changes fastest.
Arguments:
- incoming: float32 [4, 8, 4, 128, 128], P('row', 'col'), may hold values from -6 to 6
- block_map: int32 [4, 8, 4], P('row', 'col'), may hold values from 0 to 127, as said below
- panel_row: float32 [4, 4, 128, 16, 8, 128], P(None, 'row', None, None, 'col'), may hold values from -0.125 to 0.125
- diag_inverse: float32 [2, 8, 128, 128], P(None, 'col'), may hold values from -1 to 2.5
Outputs:
- panel_solution: float32 [128, 2, 8, 128], P('row', None, 'col')
- trailing_rhs: float32 [128, 14, 8, 128], P('row', None, 'col')
The draws below stay inside these ranges and needn't reach their ends.
Inputs may be any that keep to these rules, and one draw needn't show every extreme that they name: block_map names every block index from 0 to 127 exactly once; the 4 blocks of one device lie in distinct grid columns, block b lying in grid column b mod 8.
All inputs are finite; a program needn't handle non-finite values.
Results may differ from the reference program's by a relative error of at most 0.00013.
Values sent between devices are 32-bit elements; how exact they have to be, the bound alone decides.
A program may use at most 64 MiB of HBM per device.

```python
import jax
import jax.numpy as jnp
from jax import lax

NB = 128
PW = 2048
NRHS = 128
SRC_BLK = 4
ORDER = 16384
SLOTS = 16
NBLK = 128
PWB = 16
TR = 4
TC = 2
TSLOTS = 14
N_ROW = 4
N_COL = 8


def draw_block_map(key, part):
    first_key, second_key = jax.random.split(jax.random.fold_in(key, 11))
    row_keys = jax.random.split(first_key, N_ROW)
    offsets = jax.vmap(lambda subkey: jax.random.permutation(subkey, N_COL)[:SRC_BLK])(row_keys)
    devices_in = jnp.arange(N_COL, dtype=jnp.int32)
    column_of = (devices_in[None, :, None] + offsets[:, None, :]) % N_COL
    column_keys = jax.random.split(second_key, N_COL)
    orders = jax.vmap(lambda subkey: jax.random.permutation(subkey, SLOTS))(column_keys)
    entries = jnp.arange(N_ROW, dtype=jnp.int32)[:, None, None] * SRC_BLK + jnp.arange(SRC_BLK, dtype=jnp.int32)[None, None, :]
    entries = jnp.broadcast_to(entries, (N_ROW, N_COL, SRC_BLK))
    slot_of = orders[column_of, entries]
    return (slot_of * N_COL + column_of).astype(jnp.int32)


def draw_diag_inverse(key, part):
    first_key = jax.random.fold_in(jax.random.fold_in(key, 23), 0)
    identity = jnp.eye(NB, dtype=jnp.float32)
    noise = jnp.clip(jax.random.normal(first_key, (TC, N_COL, NB, NB), jnp.float32), -4.0, 4.0)
    diagonal = jnp.ones((TC, N_COL, NB, 1), jnp.float32)
    return diagonal * identity + 0.5 * noise / jnp.sqrt(jnp.float32(NB))


def block_scale(key, dims, cuts, smallest, top_value):
    def one(axis_at, blocks):
        heights = jax.random.uniform(jax.random.fold_in(jax.random.fold_in(key, 6), axis_at), (blocks,), jnp.float32, smallest / len(cuts), top_value / len(cuts))
        return jnp.repeat(jnp.exp(heights), dims[axis_at] // blocks).reshape((-1,) + (1,) * (len(dims) - axis_at - 1))

    factor_of = one(*cuts[0])
    for cut in cuts[1:]:
        factor_of = factor_of * one(*cut)
    return factor_of


def normal_values(stream_key, extent, spread, reach, cuts=(), kind=jnp.bfloat16):
    values = spread * jax.random.normal(stream_key, extent, jnp.float32)
    if cuts:
        values = values * block_scale(stream_key, extent, cuts, -0.22, 0.18)
    return jnp.clip(values, -reach, reach).astype(kind)


def setup_inputs(seed: int = 0) -> dict:
    streams_of = jax.random.split(jax.random.key(seed), 5)
    return {
        "incoming": normal_values(streams_of[0], (N_ROW, N_COL, SRC_BLK, NRHS, NB), 1.0, 6.0, ((0, 4), (1, 8)), jnp.float32),
        "block_map": draw_block_map(jax.random.fold_in(streams_of[4], 71), 0),
        "panel_row": normal_values(streams_of[2], (TR, N_ROW, NB, SLOTS, N_COL, NB), PW ** -0.5, 0.125, ((1, 4), (4, 8)), jnp.float32),
        "diag_inverse": draw_diag_inverse(jax.random.fold_in(streams_of[4], 71), 0),
    }


def reference(incoming, block_map, panel_row, diag_inverse):
    highest = lax.Precision.HIGHEST
    block_total = N_ROW * N_COL * SRC_BLK
    pieces = incoming.reshape(block_total, NRHS, NB)
    targets = block_map.reshape(block_total).astype(jnp.int32)
    placed = jnp.zeros((NBLK, NRHS, NB), jnp.float32).at[targets].set(pieces)
    rhs_rows = jnp.transpose(placed, (1, 0, 2)).reshape(NRHS, ORDER)
    upper_rows = panel_row.reshape(PW, ORDER)
    inverse = diag_inverse.reshape(PWB, NB, NB)
    solved = jnp.zeros((NRHS, PW), jnp.float32)
    for block_index in range(PWB):
        lower_edge = block_index * NB
        carried = jnp.dot(solved, upper_rows[:, lower_edge:lower_edge + NB], precision=highest, preferred_element_type=jnp.float32)
        residue = rhs_rows[:, lower_edge:lower_edge + NB] - carried
        solution_block = jnp.dot(residue, inverse[block_index].T, precision=highest, preferred_element_type=jnp.float32)
        solved = solved.at[:, lower_edge:lower_edge + NB].set(solution_block)
    update = jnp.dot(solved, upper_rows[:, PW:], precision=highest, preferred_element_type=jnp.float32)
    trailing = rhs_rows[:, PW:] - update
    return solved.reshape(NRHS, TC, N_COL, NB), trailing.reshape(NRHS, TSLOTS, N_COL, NB)
```

```python
import functools

import jax
import jax.numpy as jnp
from jax import lax
from jax.experimental import pallas as pl
from jax.experimental.pallas import tpu as pltpu
from jax.sharding import PartitionSpec as P

MESH = pl.DeviceIdType.MESH
F32 = jnp.float32
BF16 = jnp.bfloat16


def split(x):
    high = x.astype(BF16)
    return high, (x - high.astype(F32)).astype(BF16)


def dot_split(a, b, b_dim=0):
    dims = (((1,), (b_dim,)), ((), ()))

    def one(x, y):
        return lax.dot_general(x, y, dims, preferred_element_type=F32)

    a_high, a_low = a
    b_high, b_low = b
    return one(a_high, b_high) + (one(a_low, b_high) + one(a_high, b_low))


def dot3(a, b, b_dim=0):
    return dot_split(split(a), split(b), b_dim)


def kernel(sizes, bm, inc, up, inv, sol_out, tr_out, outb, recv, g, uv, yall, acc, part, rbuf, yh, yl,
           a_send, a_recv, g_send, g_recv, u_sem, y_send, y_recv, f_send, p_send, p_recv):
    NR, NC, SB, KS, NB, TR, SLOTS, TC = sizes
    PB = TR * NR
    TS = SLOTS - TC
    N = NR * NC
    r = lax.axis_index("row")
    c = lax.axis_index("col")
    me = r * NC + c

    def remote(src, dst, ssem, rsem, row, col):
        return pltpu.make_async_remote_copy(
            src_ref=src, dst_ref=dst, send_sem=ssem, recv_sem=rsem, device_id=(row, col), device_id_type=MESH)

    barrier = pltpu.get_barrier_semaphore()

    @pl.loop(1, N)
    def _(k):
        t = lax.rem(me + k, N)
        pl.semaphore_signal(barrier, inc=1, device_id=(t // NC, lax.rem(t, NC)), device_id_type=MESH)

    for s in range(TC):
        for t in range(TR):
            a = t * NR + r

            @pl.when(a < s * NC + c)
            def _(s=s, t=t, a=a):
                pltpu.make_async_copy(up.at[t, :, s, :], g.at[a, s], g_recv.at[a, s]).start()

    @pl.loop(0, TS)
    def _(s):
        pltpu.make_async_copy(up.at[:, :, TC + s, :], uv.at[s], u_sem.at[s]).start()

    @pl.loop(0, NC)
    def _(cc):
        pick = jnp.int32(0)
        label = jnp.int32(-1)
        for u in range(SB):
            b = bm[u]
            hit = lax.rem(b, NC) == cc
            pick = jnp.where(hit, u, pick)
            label = jnp.where(hit, b, label)
        outb[cc, :, :KS, :] = inc[pick]
        outb[cc, :, KS:, :] = jnp.full((NR, 8, NB), label.astype(F32), F32)

    pl.semaphore_wait(barrier, N - 1)

    def a_copy(k):
        t = lax.rem(me + k, N)
        row, col = t // NC, lax.rem(t, NC)
        return remote(outb.at[col, row], recv.at[me], a_send.at[t], a_recv.at[me], row, col)

    @pl.loop(1, N)
    def _(k):
        a_copy(k).start()

    recv[me] = outb[c, r]

    def g_copy(t, s, k):
        a = t * NR + r
        row = lax.rem(r + k, NR)
        return remote(up.at[t, :, s, :], g.at[a, s], g_send.at[t, s, k - 1], g_recv.at[a, s], row, c)

    for t in range(TR):
        for s in range(TC):
            @pl.when(t * NR + r < s * NC + c)
            def _(t=t, s=s):
                for k in range(1, NR):
                    g_copy(t, s, k).start()

    @pl.loop(1, N)
    def _(k):
        q = lax.rem(me + k, N)
        remote(recv.at[q], recv.at[q], a_send.at[q], a_recv.at[q], r, c).wait_recv()

    def rhs_of(s):
        wanted = (s * NC + c).astype(F32)

        def body(q, total):
            x = recv[q]
            hit = x[KS:] == wanted
            data = x[:KS].reshape(KS // 8, 8, NB)
            return total + jnp.where(hit[None], data, 0.0)

        return lax.fori_loop(0, N, body, jnp.zeros((KS // 8, 8, NB), F32), unroll=8).reshape(KS, NB)

    for s in range(TC):
        acc[s] = rhs_of(jnp.int32(s))

    def y_copy(i, slot, k):
        col = lax.rem(c + k, NC)
        return remote(yall.at[i, r], yall.at[i, r], y_send.at[slot, k - 1], y_recv.at[i, r], r, col)

    def f_copy(i):
        return remote(yall.at[i, r], yall.at[i, r], f_send.at[i], y_recv.at[i, r], lax.rem(i, NR), c)

    @pl.loop(0, PB)
    def _(i):
        owner = lax.rem(i, NC)
        slot = i // NC

        @pl.when(c == owner)
        def _():
            y = dot3(acc[slot], inv[slot], 1)
            yall[i, r] = y
            sol_out[slot] = y

            @pl.loop(1, NC)
            def _(k):
                y_copy(i, slot, k).start()

        @pl.when(c != owner)
        def _():
            remote(yall.at[i, r], yall.at[i, r], f_send.at[i], y_recv.at[i, r], r, c).wait_recv()

        @pl.when(lax.rem(i, NR) != r)
        def _():
            f_copy(i).start()

        for s in range(TC):
            @pl.when(i < s * NC + c)
            def _(s=s):
                pltpu.make_async_copy(g.at[i, s], g.at[i, s], g_recv.at[i, s]).wait()
                acc[s] -= dot3(yall[i, r], g[i, s])

    for t in range(TR):
        i = t * NR + r
        for k in range(1, NR):
            p = lax.rem(r + k, NR)
            remote(yall.at[i, p], yall.at[i, p], f_send.at[i], y_recv.at[i, p], r, c).wait_recv()
        high, low = split(yall[i].reshape(NR * KS, NB))
        yh[:, t * NB:(t + 1) * NB] = high
        yl[:, t * NB:(t + 1) * NB] = low

    def p_copy(s, k):
        row = lax.rem(r + k, NR)
        return remote(part.at[s, row], rbuf.at[s, k - 1], p_send.at[s, k - 1], p_recv.at[s, k - 1], row, c)

    @pl.loop(0, TS)
    def _(s):
        pltpu.make_async_copy(uv.at[s], uv.at[s], u_sem.at[s]).wait()
        product = dot_split((yh[...], yl[...]), split(uv[s].reshape(TR * NB, NB)))
        part[s] = product.reshape(NR, KS, NB)
        for k in range(1, NR):
            p_copy(s, k).start()

    @pl.loop(0, TS)
    def _(s):
        tr_out[s] = rhs_of(TC + s) - part[s, r]

    @pl.loop(0, TS)
    def _(s):
        total = tr_out[s]
        for k in range(1, NR):
            p_copy(s, k).wait_recv()
            total = total - rbuf[s, k - 1]
        tr_out[s] = total

    @pl.loop(1, N)
    def _(k):
        a_copy(k).wait_send()

    for t in range(TR):
        for s in range(TC):
            @pl.when(t * NR + r < s * NC + c)
            def _(t=t, s=s):
                for k in range(1, NR):
                    g_copy(t, s, k).wait_send()

    for s in range(TC):
        @pl.loop(1, NC)
        def _(k, s=s):
            y_copy(s * NC + c, s, k).wait_send()

    @pl.loop(0, PB)
    def _(i):
        @pl.when(lax.rem(i, NR) != r)
        def _():
            f_copy(i).wait_send()

    @pl.loop(0, TS)
    def _(s):
        for k in range(1, NR):
            p_copy(s, k).wait_send()


def per_device(incoming, block_map, panel_row, diag_inverse):
    NR = lax.axis_size("row")
    NC = lax.axis_size("col")
    SB, NRHS, NB = incoming.shape[2:]
    KS = NRHS // NR
    TR = panel_row.shape[0]
    SLOTS = panel_row.shape[3]
    TC = diag_inverse.shape[0]
    PB = TR * NR
    TS = SLOTS - TC
    N = NR * NC
    vmem = pl.BlockSpec(memory_space=pltpu.VMEM)
    dma = pltpu.SemaphoreType.DMA
    sol, trailing = pl.pallas_call(
        functools.partial(kernel, (NR, NC, SB, KS, NB, TR, SLOTS, TC)),
        out_shape=(jax.ShapeDtypeStruct((TC, KS, NB), F32), jax.ShapeDtypeStruct((TS, KS, NB), F32)),
        in_specs=[pl.BlockSpec(memory_space=pltpu.SMEM), vmem, pl.BlockSpec(memory_space=pl.ANY), vmem],
        out_specs=(vmem, vmem),
        scratch_shapes=[
            pltpu.VMEM((NC, NR, KS + 8, NB), F32),
            pltpu.VMEM((N, KS + 8, NB), F32),
            pltpu.VMEM((PB, TC, NB, NB), F32),
            pltpu.VMEM((TS, TR, NB, NB), F32),
            pltpu.VMEM((PB, NR, KS, NB), F32),
            pltpu.VMEM((TC, KS, NB), F32),
            pltpu.VMEM((TS, NR, KS, NB), F32),
            pltpu.VMEM((TS, NR - 1, KS, NB), F32),
            pltpu.VMEM((NRHS, TR * NB), BF16),
            pltpu.VMEM((NRHS, TR * NB), BF16),
            dma((N,)),
            dma((N,)),
            dma((TR, TC, NR - 1)),
            dma((PB, TC)),
            dma((TS,)),
            dma((TC, NC - 1)),
            dma((PB, NR)),
            dma((PB,)),
            dma((TS, NR - 1)),
            dma((TS, NR - 1)),
        ],
        compiler_params=pltpu.CompilerParams(
            collective_id=0, has_side_effects=True, vmem_limit_bytes=40 * 1024 * 1024),
    )(
        block_map.reshape(SB),
        incoming.reshape(SB, NR, KS, NB),
        panel_row.reshape(TR, NB, SLOTS, NB),
        diag_inverse.reshape(TC, NB, NB),
    )
    return (
        jnp.transpose(sol, (1, 0, 2))[:, :, None, :],
        jnp.transpose(trailing, (1, 0, 2))[:, :, None, :],
    )


def solution(mesh):
    in_specs = (
        P("row", "col", None, None, None),
        P("row", "col", None),
        P(None, "row", None, None, "col", None),
        P(None, "col", None, None),
    )
    out_specs = (P("row", None, "col", None), P("row", None, "col", None))
    return jax.shard_map(
        per_device, mesh=mesh, in_specs=in_specs, out_specs=out_specs, check_vma=False
    )
```

```python
import functools

import jax
import jax.numpy as jnp
from jax import lax
from jax.experimental import pallas as pl
from jax.experimental.pallas import tpu as pltpu
from jax.sharding import PartitionSpec as P

MESH = pl.DeviceIdType.MESH
F32 = jnp.float32
BF16 = jnp.bfloat16


def split(x):
    high = x.astype(BF16)
    return high, (x - high.astype(F32)).astype(BF16)


def tall(x):
    return jnp.concatenate(split(x), axis=0)


def wide(x):
    return jnp.concatenate(split(x), axis=1)


def product(a, b, b_dim=0):
    out = lax.dot_general(a, b, (((1,), (b_dim,)), ((), ())), preferred_element_type=F32)
    rows, cols = out.shape[0] // 2, out.shape[1] // 2
    return out[:rows, :cols] + (out[:rows, cols:] + out[rows:, :cols])


def kernel(sizes, bm, inc_hbm, up, inv_hbm, sol_out, tr_out, outb, recv, g, uv, yall, acc, part, rbuf, ycat, uvs,
           inc, inv, ivs, wsp, zed,
           a_send, a_recv, g_send, g_recv, u_sem, y_send, y_recv, f_send, p_send, p_recv, i_sem):
    NR, NC, SB, KS, NB, TR, SLOTS, TC = sizes
    PB = TR * NR
    TS = SLOTS - TC
    N = NR * NC
    NRHS = NR * KS
    r = lax.axis_index("row")
    c = lax.axis_index("col")
    me = r * NC + c

    def remote(src, dst, ssem, rsem, row, col):
        return pltpu.make_async_remote_copy(
            src_ref=src, dst_ref=dst, send_sem=ssem, recv_sem=rsem, device_id=(row, col), device_id_type=MESH)

    inc_copy = pltpu.make_async_copy(inc_hbm, inc, i_sem.at[0])
    inv_copy = pltpu.make_async_copy(inv_hbm, inv, i_sem.at[1])
    inc_copy.start()
    inv_copy.start()
    barrier = pltpu.get_barrier_semaphore()

    @pl.loop(1, N)
    def _(k):
        t = lax.rem(me + k, N)
        pl.semaphore_signal(barrier, inc=1, device_id=(t // NC, lax.rem(t, NC)), device_id_type=MESH)

    for s in range(TC):
        for t in range(TR):
            a = t * NR + r

            @pl.when(a < s * NC + c)
            def _(s=s, t=t, a=a):
                pltpu.make_async_copy(up.at[t, :, s, :], g.at[a, s], g_recv.at[a, s]).start()

    @pl.loop(0, TS)
    def _(s):
        pltpu.make_async_copy(up.at[:, :, TC + s, :], uv.at[s], u_sem.at[s]).start()

    inc_copy.wait()

    @pl.loop(0, NC)
    def _(cc):
        pick = jnp.int32(0)
        label = jnp.int32(-1)
        for u in range(SB):
            b = bm[u]
            hit = lax.rem(b, NC) == cc
            pick = jnp.where(hit, u, pick)
            label = jnp.where(hit, b, label)
        outb[cc, :, :KS, :] = inc[pick]
        outb[cc, :, KS:, :] = jnp.full((NR, 8, NB), label.astype(F32), F32)

    pl.semaphore_wait(barrier, N - 1)

    def a_copy(k):
        t = lax.rem(me + k, N)
        row, col = t // NC, lax.rem(t, NC)
        return remote(outb.at[col, row], recv.at[me], a_send.at[t], a_recv.at[me], row, col)

    @pl.loop(1, N)
    def _(k):
        a_copy(k).start()

    recv[me] = outb[c, r]

    def g_copy(t, s, k):
        a = t * NR + r
        row = lax.rem(r + k, NR)
        return remote(up.at[t, :, s, :], g.at[a, s], g_send.at[t, s, k - 1], g_recv.at[a, s], row, c)

    for t in range(TR):
        for s in range(TC):
            @pl.when(t * NR + r < s * NC + c)
            def _(t=t, s=s):
                for k in range(1, NR):
                    g_copy(t, s, k).start()

    inv_copy.wait()
    for s in range(TC):
        ivs[s] = tall(inv[s])

    @pl.loop(0, TS)
    def _(s):
        pltpu.make_async_copy(uv.at[s], uv.at[s], u_sem.at[s]).wait()
        uvs[s] = wide(uv[s].reshape(TR * NB, NB))

    def g_wait(i, s):
        pltpu.make_async_copy(g.at[i, s], g.at[i, s], g_recv.at[i, s]).wait()

    def prepare(s):
        before = s * NC + c - 1
        g_wait(before, s)
        wsp[s] = wide(product(tall(g[before, s]), ivs[s], 1))

    @pl.when(c > 0)
    def _():
        prepare(0)

    @pl.loop(1, N)
    def _(k):
        q = lax.rem(me + k, N)
        remote(recv.at[q], recv.at[q], a_send.at[q], a_recv.at[q], r, c).wait_recv()

    def rhs_of(s):
        wanted = (s * NC + c).astype(F32)

        def body(q, total):
            x = recv[q]
            hit = x[KS:] == wanted
            data = x[:KS].reshape(KS // 8, 8, NB)
            return total + jnp.where(hit[None], data, 0.0)

        return lax.fori_loop(0, N, body, jnp.zeros((KS // 8, 8, NB), F32), unroll=8).reshape(KS, NB)

    def y_copy(i, slot, k):
        col = lax.rem(c + k, NC)
        return remote(yall.at[i, r], yall.at[i, r], y_send.at[slot, k - 1], y_recv.at[i, r], r, col)

    def f_copy(i):
        return remote(yall.at[i, r], yall.at[i, r], f_send.at[i], y_recv.at[i, r], lax.rem(i, NR), c)

    def publish(i, slot, y):
        yall[i, r] = y

        @pl.loop(1, NC)
        def _(k):
            y_copy(i, slot, k).start()

        sol_out[slot] = y

    acc[0] = rhs_of(jnp.int32(0))

    @pl.when(c == 0)
    def _():
        publish(jnp.int32(0), 0, product(tall(acc[0]), ivs[0], 1))

    @pl.when(c == 1)
    def _():
        zed[...] = product(tall(acc[0]), ivs[0], 1)

    for s in range(1, TC):
        acc[s] = rhs_of(jnp.int32(s))

    @pl.loop(0, PB)
    def _(i):
        @pl.when(c != lax.rem(i, NC))
        def _():
            remote(yall.at[i, r], yall.at[i, r], f_send.at[i], y_recv.at[i, r], r, c).wait_recv()

        y = tall(yall[i, r])

        for s in range(TC):
            @pl.when(i + 1 == s * NC + c)
            def _(s=s):
                publish(i + 1, s, zed[...] - product(y, wsp[s]))

        @pl.when(lax.rem(i, NR) != r)
        def _():
            f_copy(i).start()

        for s in range(TC):
            @pl.when(i + 1 < s * NC + c)
            def _(s=s):
                g_wait(i, s)
                acc[s] -= product(y, wide(g[i, s]))

            @pl.when(i + 2 == s * NC + c)
            def _(s=s):
                zed[...] = product(tall(acc[s]), ivs[s], 1)

            if s > 0:
                @pl.when(i == (s - 1) * NC + c)
                def _(s=s):
                    prepare(s)

    for t in range(TR):
        i = t * NR + r
        for k in range(1, NR):
            p = lax.rem(r + k, NR)
            remote(yall.at[i, p], yall.at[i, p], f_send.at[i], y_recv.at[i, p], r, c).wait_recv()
        ycat[:, t * NB:(t + 1) * NB] = tall(yall[i].reshape(NRHS, NB))

    def p_copy(s, k):
        row = lax.rem(r + k, NR)
        return remote(part.at[s, row], rbuf.at[s, k - 1], p_send.at[s, k - 1], p_recv.at[s, k - 1], row, c)

    @pl.loop(0, TS)
    def _(s):
        part[s] = product(ycat[...], uvs[s]).reshape(NR, KS, NB)
        for k in range(1, NR):
            p_copy(s, k).start()

    @pl.loop(0, TS)
    def _(s):
        tr_out[s] = rhs_of(TC + s) - part[s, r]

    @pl.loop(0, TS)
    def _(s):
        total = tr_out[s]
        for k in range(1, NR):
            p_copy(s, k).wait_recv()
            total = total - rbuf[s, k - 1]
        tr_out[s] = total

    @pl.loop(1, N)
    def _(k):
        a_copy(k).wait_send()

    for t in range(TR):
        for s in range(TC):
            @pl.when(t * NR + r < s * NC + c)
            def _(t=t, s=s):
                for k in range(1, NR):
                    g_copy(t, s, k).wait_send()

    for s in range(TC):
        @pl.loop(1, NC)
        def _(k, s=s):
            y_copy(s * NC + c, s, k).wait_send()

    @pl.loop(0, PB)
    def _(i):
        @pl.when(lax.rem(i, NR) != r)
        def _():
            f_copy(i).wait_send()

    @pl.loop(0, TS)
    def _(s):
        for k in range(1, NR):
            p_copy(s, k).wait_send()


def per_device(incoming, block_map, panel_row, diag_inverse):
    NR = lax.axis_size("row")
    NC = lax.axis_size("col")
    SB, NRHS, NB = incoming.shape[2:]
    KS = NRHS // NR
    TR = panel_row.shape[0]
    SLOTS = panel_row.shape[3]
    TC = diag_inverse.shape[0]
    PB = TR * NR
    TS = SLOTS - TC
    N = NR * NC
    vmem = pl.BlockSpec(memory_space=pltpu.VMEM)
    dma = pltpu.SemaphoreType.DMA
    sol, trailing = pl.pallas_call(
        functools.partial(kernel, (NR, NC, SB, KS, NB, TR, SLOTS, TC)),
        out_shape=(jax.ShapeDtypeStruct((TC, KS, NB), F32), jax.ShapeDtypeStruct((TS, KS, NB), F32)),
        in_specs=[pl.BlockSpec(memory_space=pltpu.SMEM)] + [pl.BlockSpec(memory_space=pltpu.HBM)] * 3,
        out_specs=(vmem, vmem),
        scratch_shapes=[
            pltpu.VMEM((NC, NR, KS + 8, NB), F32),
            pltpu.VMEM((N, KS + 8, NB), F32),
            pltpu.VMEM((PB, TC, NB, NB), F32),
            pltpu.VMEM((TS, TR, NB, NB), F32),
            pltpu.VMEM((PB, NR, KS, NB), F32),
            pltpu.VMEM((TC, KS, NB), F32),
            pltpu.VMEM((TS, NR, KS, NB), F32),
            pltpu.VMEM((TS, NR - 1, KS, NB), F32),
            pltpu.VMEM((2 * NRHS, TR * NB), BF16),
            pltpu.VMEM((TS, TR * NB, 2 * NB), BF16),
            pltpu.VMEM((SB, NR, KS, NB), F32),
            pltpu.VMEM((TC, NB, NB), F32),
            pltpu.VMEM((TC, 2 * NB, NB), BF16),
            pltpu.VMEM((TC, NB, 2 * NB), BF16),
            pltpu.VMEM((KS, NB), F32),
            dma((N,)),
            dma((N,)),
            dma((TR, TC, NR - 1)),
            dma((PB, TC)),
            dma((TS,)),
            dma((TC, NC - 1)),
            dma((PB, NR)),
            dma((PB,)),
            dma((TS, NR - 1)),
            dma((TS, NR - 1)),
            dma((2,)),
        ],
        compiler_params=pltpu.CompilerParams(
            collective_id=0, has_side_effects=True, vmem_limit_bytes=40 * 1024 * 1024),
    )(
        block_map.reshape(SB),
        incoming.reshape(SB, NR, KS, NB),
        panel_row.reshape(TR, NB, SLOTS, NB),
        diag_inverse.reshape(TC, NB, NB),
    )
    return (
        jnp.transpose(sol, (1, 0, 2))[:, :, None, :],
        jnp.transpose(trailing, (1, 0, 2))[:, :, None, :],
    )


def solution(mesh):
    in_specs = (
        P("row", "col", None, None, None),
        P("row", "col", None),
        P(None, "row", None, None, "col", None),
        P(None, "col", None, None),
    )
    out_specs = (P("row", None, "col", None), P("row", None, "col", None))
    return jax.shard_map(
        per_device, mesh=mesh, in_specs=in_specs, out_specs=out_specs, check_vma=False
    )
```

```python
import functools

import jax
import jax.numpy as jnp
from jax import lax
from jax.experimental import pallas as pl
from jax.experimental.pallas import tpu as pltpu
from jax.sharding import PartitionSpec as P

MESH = pl.DeviceIdType.MESH
F32 = jnp.float32
BF16 = jnp.bfloat16


def split(x):
    high = x.astype(BF16)
    return high, (x - high.astype(F32)).astype(BF16)


def tall(x):
    return jnp.concatenate(split(x), axis=0)


def wide(x):
    return jnp.concatenate(split(x), axis=1)


def product(a, b, b_dim=0):
    out = lax.dot_general(a, b, (((1,), (b_dim,)), ((), ())), preferred_element_type=F32)
    rows, cols = out.shape[0] // 2, out.shape[1] // 2
    return out[:rows, :cols] + (out[:rows, cols:] + out[rows:, :cols])


def kernel(sizes, bm, inc_hbm, up, inv_hbm, sol_out, tr_out, outb, recv, g, uv, yall, acc, part, rbuf, ycat, uvs,
           inc, inv, ivs, wsp, zed, row_out, row_in, blocks_out, blocks_in,
           a_send, a_recv, g_send, g_recv, u_sem, y_send, y_recv, f_send, p_send, p_recv, i_sem, r_send, r_recv, b_send, b_recv):
    NR, NC, SB, KS, NB, TR, SLOTS, TC = sizes
    PB = TR * NR
    TS = SLOTS - TC
    N = NR * NC
    NRHS = NR * KS
    r = lax.axis_index("row")
    c = lax.axis_index("col")
    me = r * NC + c

    def remote(src, dst, ssem, rsem, row, col):
        return pltpu.make_async_remote_copy(
            src_ref=src, dst_ref=dst, send_sem=ssem, recv_sem=rsem, device_id=(row, col), device_id_type=MESH)

    inc_copy = pltpu.make_async_copy(inc_hbm, inc, i_sem.at[0])
    inv_copy = pltpu.make_async_copy(inv_hbm, inv, i_sem.at[1])
    inc_copy.start()
    inv_copy.start()
    barrier = pltpu.get_barrier_semaphore()

    @pl.loop(1, N)
    def _(k):
        t = lax.rem(me + k, N)
        pl.semaphore_signal(barrier, inc=1, device_id=(t // NC, lax.rem(t, NC)), device_id_type=MESH)

    for s in range(TC):
        for t in range(TR):
            a = t * NR + r

            @pl.when(a < s * NC + c)
            def _(s=s, t=t, a=a):
                pltpu.make_async_copy(up.at[t, :, s, :], g.at[a, s], g_recv.at[a, s]).start()

    @pl.loop(0, TS)
    def _(s):
        pltpu.make_async_copy(up.at[:, :, TC + s, :], uv.at[s], u_sem.at[s]).start()

    inc_copy.wait()

    for u in range(SB):
        row_out[:, u, :KS, :] = inc[u]
        row_out[:, u, KS:, :] = jnp.full((NR, 8, NB), bm[u].astype(F32), F32)
    row_in[r] = row_out[r]

    pl.semaphore_wait(barrier, N - 1)

    def a_copy(k):
        t = lax.rem(me + k, N)
        row, col = t // NC, lax.rem(t, NC)
        return remote(outb.at[col, row], recv.at[me], a_send.at[t], a_recv.at[me], row, col)

    def r_copy(k):
        row = lax.rem(r + k, NR)
        return remote(row_out.at[row], row_in.at[r], r_send.at[k - 1], r_recv.at[r], row, c)

    for k in range(1, NR):
        r_copy(k).start()

    def g_copy(t, s, k):
        a = t * NR + r
        row = lax.rem(r + k, NR)
        return remote(up.at[t, :, s, :], g.at[a, s], g_send.at[t, s, k - 1], g_recv.at[a, s], row, c)

    for t in range(TR):
        for s in range(TC):
            @pl.when(t * NR + r < s * NC + c)
            def _(t=t, s=s):
                for k in range(1, NR):
                    g_copy(t, s, k).start()

    inv_copy.wait()
    for s in range(TC):
        ivs[s] = tall(inv[s])

    @pl.loop(0, NC)
    def _(cc):
        pick = jnp.int32(0)
        label = jnp.int32(-1)
        for u in range(SB):
            b = bm[u]
            hit = lax.rem(b, NC) == cc
            pick = jnp.where(hit, u, pick)
            label = jnp.where(hit, b, label)
        outb[cc, :, :KS, :] = inc[pick]
        outb[cc, :, KS:, :] = jnp.full((NR, 8, NB), label.astype(F32), F32)

    recv[me] = outb[c, r]

    for k in range(1, NR):
        row = lax.rem(r + k, NR)
        remote(row_in.at[row], row_in.at[row], r_send.at[k - 1], r_recv.at[row], r, c).wait_recv()

    def pick(source, count, block):
        wanted = block.astype(F32)

        def body(q, total):
            x = source(q)
            hit = x[KS:] == wanted
            data = x[:KS].reshape(KS // 8, 8, NB)
            return total + jnp.where(hit[None], data, 0.0)

        zeros = jnp.zeros((KS // 8, 8, NB), F32)
        return lax.fori_loop(0, count, body, zeros, unroll=8).reshape(KS, NB)

    def b_copy(s, k):
        col = lax.rem(c + k, NC)
        return remote(blocks_out.at[s, col], blocks_in.at[s, c], b_send.at[s, k - 1], b_recv.at[s, c], r, col)

    for s in range(TC):
        @pl.loop(1, NC)
        def _(k, s=s):
            col = lax.rem(c + k, NC)
            blocks_out[s, col] = pick(lambda q: row_in[q // SB, lax.rem(q, SB)], NR * SB, s * NC + col)
            b_copy(s, k).start()

        blocks_in[s, c] = pick(lambda q: row_in[q // SB, lax.rem(q, SB)], NR * SB, s * NC + c)

    def panel_rhs(s):
        @pl.loop(1, NC)
        def _(k):
            q = lax.rem(c + k, NC)
            remote(blocks_in.at[s, q], blocks_in.at[s, q], b_send.at[s, k - 1], b_recv.at[s, q], r, c).wait_recv()

        return jnp.sum(blocks_in[s], axis=0)

    @pl.loop(0, TS)
    def _(s):
        pltpu.make_async_copy(uv.at[s], uv.at[s], u_sem.at[s]).wait()
        uvs[s] = wide(uv[s].reshape(TR * NB, NB))

    def g_wait(i, s):
        pltpu.make_async_copy(g.at[i, s], g.at[i, s], g_recv.at[i, s]).wait()

    def prepare(s):
        before = s * NC + c - 1
        g_wait(before, s)
        wsp[s] = wide(product(tall(g[before, s]), ivs[s], 1))

    @pl.when(c > 0)
    def _():
        prepare(0)

    def rhs_of(s):
        return pick(lambda q: recv[q], N, s * NC + c)

    def y_copy(i, slot, k):
        col = lax.rem(c + k, NC)
        return remote(yall.at[i, r], yall.at[i, r], y_send.at[slot, k - 1], y_recv.at[i, r], r, col)

    def f_copy(i):
        return remote(yall.at[i, r], yall.at[i, r], f_send.at[i], y_recv.at[i, r], lax.rem(i, NR), c)

    def publish(i, slot, y):
        yall[i, r] = y

        @pl.loop(1, NC)
        def _(k):
            y_copy(i, slot, k).start()

        sol_out[slot] = y

    acc[0] = panel_rhs(0)

    @pl.when(c == 0)
    def _():
        publish(jnp.int32(0), 0, product(tall(acc[0]), ivs[0], 1))

    @pl.when(c == 1)
    def _():
        zed[...] = product(tall(acc[0]), ivs[0], 1)

    for s in range(1, TC):
        acc[s] = panel_rhs(s)

    @pl.loop(0, PB)
    def _(i):
        @pl.when(c != lax.rem(i, NC))
        def _():
            remote(yall.at[i, r], yall.at[i, r], f_send.at[i], y_recv.at[i, r], r, c).wait_recv()

        y = tall(yall[i, r])

        for s in range(TC):
            @pl.when(i + 1 == s * NC + c)
            def _(s=s):
                publish(i + 1, s, zed[...] - product(y, wsp[s]))

        @pl.when(lax.rem(i, NR) != r)
        def _():
            f_copy(i).start()

        for s in range(TC):
            @pl.when(i + 1 < s * NC + c)
            def _(s=s):
                g_wait(i, s)
                acc[s] -= product(y, wide(g[i, s]))

            @pl.when(i + 2 == s * NC + c)
            def _(s=s):
                zed[...] = product(tall(acc[s]), ivs[s], 1)

            if s > 0:
                @pl.when(i == (s - 1) * NC + c)
                def _(s=s):
                    prepare(s)

        for j in range(-(-N // PB)):
            k = i * -(-N // PB) + j + 1

            @pl.when(k < N)
            def _(k=k):
                a_copy(k).start()

    for t in range(TR):
        i = t * NR + r
        for k in range(1, NR):
            p = lax.rem(r + k, NR)
            remote(yall.at[i, p], yall.at[i, p], f_send.at[i], y_recv.at[i, p], r, c).wait_recv()
        ycat[:, t * NB:(t + 1) * NB] = tall(yall[i].reshape(NRHS, NB))

    def p_copy(s, k):
        row = lax.rem(r + k, NR)
        return remote(part.at[s, row], rbuf.at[s, k - 1], p_send.at[s, k - 1], p_recv.at[s, k - 1], row, c)

    @pl.loop(0, TS)
    def _(s):
        part[s] = product(ycat[...], uvs[s]).reshape(NR, KS, NB)
        for k in range(1, NR):
            p_copy(s, k).start()

    @pl.loop(1, N)
    def _(k):
        q = lax.rem(me + k, N)
        remote(recv.at[q], recv.at[q], a_send.at[q], a_recv.at[q], r, c).wait_recv()

    @pl.loop(0, TS)
    def _(s):
        tr_out[s] = rhs_of(TC + s) - part[s, r]

    @pl.loop(0, TS)
    def _(s):
        total = tr_out[s]
        for k in range(1, NR):
            p_copy(s, k).wait_recv()
            total = total - rbuf[s, k - 1]
        tr_out[s] = total

    for k in range(1, NR):
        r_copy(k).wait_send()

    for s in range(TC):
        @pl.loop(1, NC)
        def _(k, s=s):
            b_copy(s, k).wait_send()

    @pl.loop(1, N)
    def _(k):
        a_copy(k).wait_send()

    for t in range(TR):
        for s in range(TC):
            @pl.when(t * NR + r < s * NC + c)
            def _(t=t, s=s):
                for k in range(1, NR):
                    g_copy(t, s, k).wait_send()

    for s in range(TC):
        @pl.loop(1, NC)
        def _(k, s=s):
            y_copy(s * NC + c, s, k).wait_send()

    @pl.loop(0, PB)
    def _(i):
        @pl.when(lax.rem(i, NR) != r)
        def _():
            f_copy(i).wait_send()

    @pl.loop(0, TS)
    def _(s):
        for k in range(1, NR):
            p_copy(s, k).wait_send()


def per_device(incoming, block_map, panel_row, diag_inverse):
    NR = lax.axis_size("row")
    NC = lax.axis_size("col")
    SB, NRHS, NB = incoming.shape[2:]
    KS = NRHS // NR
    TR = panel_row.shape[0]
    SLOTS = panel_row.shape[3]
    TC = diag_inverse.shape[0]
    PB = TR * NR
    TS = SLOTS - TC
    N = NR * NC
    vmem = pl.BlockSpec(memory_space=pltpu.VMEM)
    dma = pltpu.SemaphoreType.DMA
    sol, trailing = pl.pallas_call(
        functools.partial(kernel, (NR, NC, SB, KS, NB, TR, SLOTS, TC)),
        out_shape=(jax.ShapeDtypeStruct((TC, KS, NB), F32), jax.ShapeDtypeStruct((TS, KS, NB), F32)),
        in_specs=[pl.BlockSpec(memory_space=pltpu.SMEM)] + [pl.BlockSpec(memory_space=pltpu.HBM)] * 3,
        out_specs=(vmem, vmem),
        scratch_shapes=[
            pltpu.VMEM((NC, NR, KS + 8, NB), F32),
            pltpu.VMEM((N, KS + 8, NB), F32),
            pltpu.VMEM((PB, TC, NB, NB), F32),
            pltpu.VMEM((TS, TR, NB, NB), F32),
            pltpu.VMEM((PB, NR, KS, NB), F32),
            pltpu.VMEM((TC, KS, NB), F32),
            pltpu.VMEM((TS, NR, KS, NB), F32),
            pltpu.VMEM((TS, NR - 1, KS, NB), F32),
            pltpu.VMEM((2 * NRHS, TR * NB), BF16),
            pltpu.VMEM((TS, TR * NB, 2 * NB), BF16),
            pltpu.VMEM((SB, NR, KS, NB), F32),
            pltpu.VMEM((TC, NB, NB), F32),
            pltpu.VMEM((TC, 2 * NB, NB), BF16),
            pltpu.VMEM((TC, NB, 2 * NB), BF16),
            pltpu.VMEM((KS, NB), F32),
            pltpu.VMEM((NR, SB, KS + 8, NB), F32),
            pltpu.VMEM((NR, SB, KS + 8, NB), F32),
            pltpu.VMEM((TC, NC, KS, NB), F32),
            pltpu.VMEM((TC, NC, KS, NB), F32),
            dma((N,)),
            dma((N,)),
            dma((TR, TC, NR - 1)),
            dma((PB, TC)),
            dma((TS,)),
            dma((TC, NC - 1)),
            dma((PB, NR)),
            dma((PB,)),
            dma((TS, NR - 1)),
            dma((TS, NR - 1)),
            dma((2,)),
            dma((NR - 1,)),
            dma((NR,)),
            dma((TC, NC - 1)),
            dma((TC, NC)),
        ],
        compiler_params=pltpu.CompilerParams(
            collective_id=0, has_side_effects=True, vmem_limit_bytes=60 * 1024 * 1024),
    )(
        block_map.reshape(SB),
        incoming.reshape(SB, NR, KS, NB),
        panel_row.reshape(TR, NB, SLOTS, NB),
        diag_inverse.reshape(TC, NB, NB),
    )
    return (
        jnp.transpose(sol, (1, 0, 2))[:, :, None, :],
        jnp.transpose(trailing, (1, 0, 2))[:, :, None, :],
    )


def solution(mesh):
    in_specs = (
        P("row", "col", None, None, None),
        P("row", "col", None),
        P(None, "row", None, None, "col", None),
        P(None, "col", None, None),
    )
    out_specs = (P("row", None, "col", None), P("row", None, "col", None))
    return jax.shard_map(
        per_device, mesh=mesh, in_specs=in_specs, out_specs=out_specs, check_vma=False
    )
```

```python
import functools

import jax
import jax.numpy as jnp
from jax import lax
from jax.experimental import pallas as pl
from jax.experimental.pallas import tpu as pltpu
from jax.sharding import PartitionSpec as P

MESH = pl.DeviceIdType.MESH
F32 = jnp.float32
BF16 = jnp.bfloat16


def split(x):
    high = x.astype(BF16)
    return high, (x - high.astype(F32)).astype(BF16)


def tall(x):
    return jnp.concatenate(split(x), axis=0)


def wide(x):
    return jnp.concatenate(split(x), axis=1)


def product(a, b, b_dim=0):
    out = lax.dot_general(a, b, (((1,), (b_dim,)), ((), ())), preferred_element_type=F32)
    rows, cols = out.shape[0] // 2, out.shape[1] // 2
    return out[:rows, :cols] + (out[:rows, cols:] + out[rows:, :cols])


def kernel(sizes, bm, inc_hbm, up, inv_hbm, sol_out, tr_out, outb, recv, g, uv, yall, acc, part, rbuf, ycat, uvs,
           inc, inv, ivs, wsp, zed, row_out, row_in, blocks_out, blocks_in,
           a_send, a_recv, g_send, g_recv, u_sem, y_send, y_recv, f_send, p_send, p_recv, i_sem, r_send, r_recv, b_send, b_recv):
    NR, NC, SB, KS, NB, TR, SLOTS, TC = sizes
    PB = TR * NR
    TS = SLOTS - TC
    N = NR * NC
    NRHS = NR * KS
    r = lax.axis_index("row")
    c = lax.axis_index("col")

    def remote(src, dst, ssem, rsem, row, col):
        return pltpu.make_async_remote_copy(
            src_ref=src, dst_ref=dst, send_sem=ssem, recv_sem=rsem, device_id=(row, col), device_id_type=MESH)

    inc_copy = pltpu.make_async_copy(inc_hbm, inc, i_sem.at[0])
    inv_copy = pltpu.make_async_copy(inv_hbm, inv, i_sem.at[1])
    inc_copy.start()
    inv_copy.start()
    barrier = pltpu.get_barrier_semaphore()

    for k in range(1, NR):
        pl.semaphore_signal(barrier, inc=1, device_id=(lax.rem(r + k, NR), c), device_id_type=MESH)
    for k in range(1, NC):
        pl.semaphore_signal(barrier, inc=1, device_id=(r, lax.rem(c + k, NC)), device_id_type=MESH)

    for s in range(TC):
        for t in range(TR):
            a = t * NR + r

            @pl.when(a < s * NC + c)
            def _(s=s, t=t, a=a):
                pltpu.make_async_copy(up.at[t, :, s, :], g.at[a, s], g_recv.at[a, s]).start()

    @pl.loop(0, TS)
    def _(s):
        pltpu.make_async_copy(up.at[:, :, TC + s, :], uv.at[s], u_sem.at[s]).start()

    inc_copy.wait()

    for u in range(SB):
        row_out[:, u, :KS, :] = inc[u]
        row_out[:, u, KS:, :] = jnp.full((NR, 8, NB), bm[u].astype(F32), F32)
    row_in[r] = row_out[r]

    pl.semaphore_wait(barrier, NR + NC - 2)

    def a_copy(k):
        col = lax.rem(c + k, NC)
        return remote(outb.at[col], recv.at[c], a_send.at[k - 1], a_recv.at[c], r, col)

    def a_wait(k):
        q = lax.rem(c + k, NC)
        remote(recv.at[q], recv.at[q], a_send.at[k - 1], a_recv.at[q], r, c).wait_recv()

    def r_copy(k):
        row = lax.rem(r + k, NR)
        return remote(row_out.at[row], row_in.at[r], r_send.at[k - 1], r_recv.at[r], row, c)

    for k in range(1, NR):
        r_copy(k).start()

    def g_copy(t, s, k):
        a = t * NR + r
        row = lax.rem(r + k, NR)
        return remote(up.at[t, :, s, :], g.at[a, s], g_send.at[t, s, k - 1], g_recv.at[a, s], row, c)

    for t in range(TR):
        for s in range(TC):
            @pl.when(t * NR + r < s * NC + c)
            def _(t=t, s=s):
                for k in range(1, NR):
                    g_copy(t, s, k).start()

    inv_copy.wait()
    for s in range(TC):
        ivs[s] = tall(inv[s])

    for k in range(1, NR):
        row = lax.rem(r + k, NR)
        remote(row_in.at[row], row_in.at[row], r_send.at[k - 1], r_recv.at[row], r, c).wait_recv()

    def pick(source, count, block):
        wanted = block.astype(F32)

        def body(q, total):
            x = source(q)
            hit = x[KS:] == wanted
            data = x[:KS].reshape(KS // 8, 8, NB)
            return total + jnp.where(hit[None], data, 0.0)

        zeros = jnp.zeros((KS // 8, 8, NB), F32)
        return lax.fori_loop(0, count, body, zeros, unroll=8).reshape(KS, NB)

    def b_copy(s, k):
        col = lax.rem(c + k, NC)
        return remote(blocks_out.at[s, col], blocks_in.at[s, c], b_send.at[s, k - 1], b_recv.at[s, c], r, col)

    for s in range(TC):
        @pl.loop(1, NC)
        def _(k, s=s):
            col = lax.rem(c + k, NC)
            blocks_out[s, col] = pick(lambda q: row_in[q // SB, lax.rem(q, SB)], NR * SB, s * NC + col)
            b_copy(s, k).start()

        blocks_in[s, c] = pick(lambda q: row_in[q // SB, lax.rem(q, SB)], NR * SB, s * NC + c)

    def panel_rhs(s):
        @pl.loop(1, NC)
        def _(k):
            q = lax.rem(c + k, NC)
            remote(blocks_in.at[s, q], blocks_in.at[s, q], b_send.at[s, k - 1], b_recv.at[s, q], r, c).wait_recv()

        return jnp.sum(blocks_in[s], axis=0)

    @pl.loop(0, NC)
    def _(cc):
        wanted = cc.astype(F32)
        for p in range(NR):
            data = jnp.zeros((KS // 8, 8, NB), F32)
            label = jnp.full((8, NB), -1.0, F32)
            for u in range(SB):
                x = row_in[p, u]
                index = x[KS:]
                hit = index - NC * jnp.floor((index + 0.5) * (1.0 / NC)) == wanted
                data = jnp.where(hit[None], x[:KS].reshape(KS // 8, 8, NB), data)
                label = jnp.where(hit, index, label)
            outb[cc, p, :KS, :] = data.reshape(KS, NB)
            outb[cc, p, KS:, :] = label

    recv[c] = outb[c]

    @pl.loop(0, TS)
    def _(s):
        pltpu.make_async_copy(uv.at[s], uv.at[s], u_sem.at[s]).wait()
        uvs[s] = wide(uv[s].reshape(TR * NB, NB))

    def g_wait(i, s):
        pltpu.make_async_copy(g.at[i, s], g.at[i, s], g_recv.at[i, s]).wait()

    def prepare(s):
        before = s * NC + c - 1
        g_wait(before, s)
        wsp[s] = wide(product(tall(g[before, s]), ivs[s], 1))

    @pl.when(c > 0)
    def _():
        prepare(0)

    def rhs_of(s):
        return pick(lambda q: recv[q // NR, lax.rem(q, NR)], N, s * NC + c)

    def y_copy(i, slot, k):
        col = lax.rem(c + k, NC)
        return remote(yall.at[i, r], yall.at[i, r], y_send.at[slot, k - 1], y_recv.at[i, r], r, col)

    def f_copy(i):
        return remote(yall.at[i, r], yall.at[i, r], f_send.at[i], y_recv.at[i, r], lax.rem(i, NR), c)

    def publish(i, slot, y):
        yall[i, r] = y

        @pl.loop(1, NC)
        def _(k):
            y_copy(i, slot, k).start()

        sol_out[slot] = y

    acc[0] = panel_rhs(0)

    @pl.when(c == 0)
    def _():
        publish(jnp.int32(0), 0, product(tall(acc[0]), ivs[0], 1))

    @pl.when(c == 1)
    def _():
        zed[...] = product(tall(acc[0]), ivs[0], 1)

    for s in range(1, TC):
        acc[s] = panel_rhs(s)

    @pl.loop(0, PB)
    def _(i):
        @pl.when(c != lax.rem(i, NC))
        def _():
            remote(yall.at[i, r], yall.at[i, r], f_send.at[i], y_recv.at[i, r], r, c).wait_recv()

        y = tall(yall[i, r])

        for s in range(TC):
            @pl.when(i + 1 == s * NC + c)
            def _(s=s):
                publish(i + 1, s, zed[...] - product(y, wsp[s]))

        @pl.when(lax.rem(i, NR) != r)
        def _():
            f_copy(i).start()

        for s in range(TC):
            @pl.when(i + 1 < s * NC + c)
            def _(s=s):
                g_wait(i, s)
                acc[s] -= product(y, wide(g[i, s]))

            @pl.when(i + 2 == s * NC + c)
            def _(s=s):
                zed[...] = product(tall(acc[s]), ivs[s], 1)

            if s > 0:
                @pl.when(i == (s - 1) * NC + c)
                def _(s=s):
                    prepare(s)

        for j in range(-(-NC // PB)):
            k = i * -(-NC // PB) + j + 1

            @pl.when(k < NC)
            def _(k=k):
                a_copy(k).start()

    for t in range(TR):
        i = t * NR + r
        for k in range(1, NR):
            p = lax.rem(r + k, NR)
            remote(yall.at[i, p], yall.at[i, p], f_send.at[i], y_recv.at[i, p], r, c).wait_recv()
        ycat[:, t * NB:(t + 1) * NB] = tall(yall[i].reshape(NRHS, NB))

    def p_copy(s, k):
        row = lax.rem(r + k, NR)
        return remote(part.at[s, row], rbuf.at[s, k - 1], p_send.at[s, k - 1], p_recv.at[s, k - 1], row, c)

    @pl.loop(0, TS)
    def _(s):
        part[s] = product(ycat[...], uvs[s]).reshape(NR, KS, NB)
        for k in range(1, NR):
            p_copy(s, k).start()

    @pl.loop(1, NC)
    def _(k):
        a_wait(k)

    @pl.loop(0, TS)
    def _(s):
        tr_out[s] = rhs_of(TC + s) - part[s, r]

    @pl.loop(0, TS)
    def _(s):
        total = tr_out[s]
        for k in range(1, NR):
            p_copy(s, k).wait_recv()
            total = total - rbuf[s, k - 1]
        tr_out[s] = total

    for k in range(1, NR):
        r_copy(k).wait_send()

    for s in range(TC):
        @pl.loop(1, NC)
        def _(k, s=s):
            b_copy(s, k).wait_send()

    @pl.loop(1, NC)
    def _(k):
        a_copy(k).wait_send()

    for t in range(TR):
        for s in range(TC):
            @pl.when(t * NR + r < s * NC + c)
            def _(t=t, s=s):
                for k in range(1, NR):
                    g_copy(t, s, k).wait_send()

    for s in range(TC):
        @pl.loop(1, NC)
        def _(k, s=s):
            y_copy(s * NC + c, s, k).wait_send()

    @pl.loop(0, PB)
    def _(i):
        @pl.when(lax.rem(i, NR) != r)
        def _():
            f_copy(i).wait_send()

    @pl.loop(0, TS)
    def _(s):
        for k in range(1, NR):
            p_copy(s, k).wait_send()


def per_device(incoming, block_map, panel_row, diag_inverse):
    NR = lax.axis_size("row")
    NC = lax.axis_size("col")
    SB, NRHS, NB = incoming.shape[2:]
    KS = NRHS // NR
    TR = panel_row.shape[0]
    SLOTS = panel_row.shape[3]
    TC = diag_inverse.shape[0]
    PB = TR * NR
    TS = SLOTS - TC
    N = NR * NC
    vmem = pl.BlockSpec(memory_space=pltpu.VMEM)
    dma = pltpu.SemaphoreType.DMA
    sol, trailing = pl.pallas_call(
        functools.partial(kernel, (NR, NC, SB, KS, NB, TR, SLOTS, TC)),
        out_shape=(jax.ShapeDtypeStruct((TC, KS, NB), F32), jax.ShapeDtypeStruct((TS, KS, NB), F32)),
        in_specs=[pl.BlockSpec(memory_space=pltpu.SMEM)] + [pl.BlockSpec(memory_space=pltpu.HBM)] * 3,
        out_specs=(vmem, vmem),
        scratch_shapes=[
            pltpu.VMEM((NC, NR, KS + 8, NB), F32),
            pltpu.VMEM((NC, NR, KS + 8, NB), F32),
            pltpu.VMEM((PB, TC, NB, NB), F32),
            pltpu.VMEM((TS, TR, NB, NB), F32),
            pltpu.VMEM((PB, NR, KS, NB), F32),
            pltpu.VMEM((TC, KS, NB), F32),
            pltpu.VMEM((TS, NR, KS, NB), F32),
            pltpu.VMEM((TS, NR - 1, KS, NB), F32),
            pltpu.VMEM((2 * NRHS, TR * NB), BF16),
            pltpu.VMEM((TS, TR * NB, 2 * NB), BF16),
            pltpu.VMEM((SB, NR, KS, NB), F32),
            pltpu.VMEM((TC, NB, NB), F32),
            pltpu.VMEM((TC, 2 * NB, NB), BF16),
            pltpu.VMEM((TC, NB, 2 * NB), BF16),
            pltpu.VMEM((KS, NB), F32),
            pltpu.VMEM((NR, SB, KS + 8, NB), F32),
            pltpu.VMEM((NR, SB, KS + 8, NB), F32),
            pltpu.VMEM((TC, NC, KS, NB), F32),
            pltpu.VMEM((TC, NC, KS, NB), F32),
            dma((NC - 1,)),
            dma((NC,)),
            dma((TR, TC, NR - 1)),
            dma((PB, TC)),
            dma((TS,)),
            dma((TC, NC - 1)),
            dma((PB, NR)),
            dma((PB,)),
            dma((TS, NR - 1)),
            dma((TS, NR - 1)),
            dma((2,)),
            dma((NR - 1,)),
            dma((NR,)),
            dma((TC, NC - 1)),
            dma((TC, NC)),
        ],
        compiler_params=pltpu.CompilerParams(
            collective_id=0, has_side_effects=True, vmem_limit_bytes=60 * 1024 * 1024),
    )(
        block_map.reshape(SB),
        incoming.reshape(SB, NR, KS, NB),
        panel_row.reshape(TR, NB, SLOTS, NB),
        diag_inverse.reshape(TC, NB, NB),
    )
    return (
        jnp.transpose(sol, (1, 0, 2))[:, :, None, :],
        jnp.transpose(trailing, (1, 0, 2))[:, :, None, :],
    )


def solution(mesh):
    in_specs = (
        P("row", "col", None, None, None),
        P("row", "col", None),
        P(None, "row", None, None, "col", None),
        P(None, "col", None, None),
    )
    out_specs = (P("row", None, "col", None), P("row", None, "col", None))
    return jax.shard_map(
        per_device, mesh=mesh, in_specs=in_specs, out_specs=out_specs, check_vma=False
    )
```
